32 devices in a mesh: inv: 2 (over x), row: 16 (over z, y, core).
Axes of the slice: x: 2, y: 2, z: 4, core: 2. Of those that a mesh axis runs over, the one named last changes fastest.
Arguments:
- rhs_data: float32 [64, 16, 128], P(('inv', 'row')), parts along dimension 0, may hold values from -720 to 720, as said below
- blocks: bfloat16 [12288, 128, 128], P(('inv', 'row')), parts along dimension 0, may hold values from -0.0390625 to 0.0390625
- block_row: int32 [12288], P(('inv', 'row')), parts along dimension 0, may hold values from 0 to 1
- block_col: int32 [12288], P(('inv', 'row')), parts along dimension 0, may hold values from 0 to 31
Outputs:
- model_update: float32 [64, 16, 128], P(('inv', 'row')), parts along dimension 0
- next_search: float32 [64, 16, 128], P(('inv', 'row')), parts along dimension 0
The draws below stay inside these ranges and needn't reach their ends.
There are 2 independent parts, one for each index of `inv`. The reference program is written for one: setup_inputs(seed, part) draws one part's arguments, and reference() takes and returns one part's arrays. A program takes and returns all parts, laid end to end along the dimension named above; each array names one. Nothing has to cross between parts.
Inputs may be any that keep to these rules, and one draw needn't show every extreme that they name: `rhs_data`: each entry is a draw times a row scale, a right-hand side scale and a factor that rises with the data block.
All inputs are finite; a program needn't handle non-finite values.
Results may differ from the reference program's by a relative error of at most 0.0051.
Values may be sent and summed in bfloat16 or wider, within the bound.
A program may use at most 64 MiB of HBM per device.

```python
import math
import jax
import jax.numpy as jnp
from jax import lax

BLK = 128
RHS = 16
DB_DEV = 2
K_DEV = 384
DB = 32
CB = 32
KB = 6144
CELLS = 4096
N_ROW = 16


def draw_rhs_data(key, part):
    key = jax.random.fold_in(key, 11)
    key_base, key_rows, key_cols = jax.random.split(key, 3)
    row_scale = jnp.exp(jax.random.uniform(key_rows, (DB, 1, BLK), jnp.float32, 0.0, math.log(10.0)))
    col_scale = jnp.exp(jax.random.uniform(key_cols, (1, RHS, 1), jnp.float32, 0.0, math.log(4.0)))
    ramp = 1.0 + 2.0 * jnp.arange(DB, dtype=jnp.float32) / max(DB - 1, 1)
    base = jax.random.normal(key_base, (DB, RHS, BLK), jnp.float32)
    base = jnp.clip(base, -6.0, 6.0)
    return base * row_scale * col_scale * ramp[:, None, None]


def touch_ends(values, own_key, least, high):
    index_at = [jax.random.randint(jax.random.fold_in(own_key, axis), (), 0, length) for axis, length in enumerate(values.shape)]
    longest = values.shape.index(max(values.shape))
    beside = index_at[:longest] + [(index_at[longest] + 1) % values.shape[longest]] + index_at[longest + 1:]
    return values.at[tuple(index_at)].set(least).at[tuple(beside)].set(high)


def levels(key, shape, cuts, low, largest):
    def one(dim, blocks):
        heights = jax.random.uniform(jax.random.fold_in(jax.random.fold_in(key, 6), dim), (blocks,), jnp.float32, low / len(cuts), largest / len(cuts))
        return jnp.repeat(jnp.exp(heights), shape[dim] // blocks).reshape((-1,) + (1,) * (len(shape) - dim - 1))

    factor_of = one(*cuts[0])
    for cut in cuts[1:]:
        factor_of = factor_of * one(*cut)
    return factor_of


def noise(stream_key, extent, width, reach, cuts=(), held_as=jnp.bfloat16):
    result = jax.random.normal(stream_key, extent, jnp.float32) * width
    if len(cuts) > 0:
        result = levels(stream_key, extent, cuts, -0.22, 0.18) * result
    return jnp.clip(result, min=-reach, max=reach).astype(held_as)


def setup_inputs(seed: int = 0, part: int = 0) -> dict:
    arg_keys = jax.random.split(jax.random.key(seed), 5)
    own_keys = jax.random.split(jax.random.fold_in(arg_keys[4], part), 5)
    return {
        "rhs_data": draw_rhs_data(jax.random.fold_in(jax.random.fold_in(arg_keys[4], part), 71), part),
        "blocks": noise(own_keys[1], (KB, BLK, BLK), (BLK * K_DEV // DB_DEV) ** -0.5, 0.0390625, ((0, 16),)),
        "block_row": touch_ends(jax.random.randint(own_keys[2], (KB,), 0, DB_DEV), jax.random.fold_in(own_keys[2], 1), 0, DB_DEV - 1).astype(jnp.int32),
        "block_col": touch_ends(jax.random.randint(own_keys[3], (KB,), 0, CB), jax.random.fold_in(own_keys[3], 1), 0, CB - 1).astype(jnp.int32),
    }


epsilon = 1e-06

def column_norm(field):
    return jnp.sqrt(lax.optimization_barrier(jnp.sum(field * field, axis=(0, 2))) + epsilon)

def forward_product(cell_bf, blocks, block_row, block_col):
    blocks_dev = blocks.reshape(N_ROW, K_DEV, BLK, BLK)
    rows_dev = block_row.reshape(N_ROW, K_DEV)
    cols_dev = block_col.reshape(N_ROW, K_DEV)

    def step(carry, item):
        blk, rows, cols = item
        picked = cell_bf[cols].astype(jnp.float32)
        prod = jnp.einsum('krj,kij->kri', picked, blk.astype(jnp.float32), precision=lax.Precision.HIGHEST)
        return (carry, jax.ops.segment_sum(prod, rows, num_segments=DB_DEV))
    _, outs = lax.scan(step, jnp.zeros((), jnp.float32), (blocks_dev, rows_dev, cols_dev))
    return outs.reshape(DB, RHS, BLK)

def transpose_product(data_bf, blocks, block_row, block_col):
    blocks_dev = blocks.reshape(N_ROW, K_DEV, BLK, BLK)
    rows_dev = block_row.reshape(N_ROW, K_DEV)
    cols_dev = block_col.reshape(N_ROW, K_DEV)
    data_dev = data_bf.reshape(N_ROW, DB_DEV, RHS, BLK)

    def step(total, item):
        blk, rows, cols, local = item
        picked = local[rows].astype(jnp.float32)
        prod = jnp.einsum('kri,kij->krj', picked, blk.astype(jnp.float32), precision=lax.Precision.HIGHEST)
        return (total.at[cols].add(prod), None)
    total, _ = lax.scan(step, jnp.zeros((CB, RHS, BLK), jnp.float32), (blocks_dev, rows_dev, cols_dev, data_dev))
    return total

def reference(rhs_data, blocks, block_row, block_col):
    beta_one = column_norm(rhs_data)
    data_dir = rhs_data / beta_one[None, :, None]
    back_one = transpose_product(data_dir.astype(jnp.bfloat16), blocks, block_row, block_col)
    alpha_one = column_norm(back_one)
    cell_dir = back_one / alpha_one[None, :, None]
    forward = forward_product(cell_dir.astype(jnp.bfloat16), blocks, block_row, block_col) - alpha_one[None, :, None] * data_dir
    beta_two = column_norm(forward)
    data_next = forward / beta_two[None, :, None]
    back_two = transpose_product(data_next.astype(jnp.bfloat16), blocks, block_row, block_col) - beta_two[None, :, None] * cell_dir
    alpha_two = column_norm(back_two)
    cell_next = back_two / alpha_two[None, :, None]
    rho = jnp.sqrt(alpha_one * alpha_one + beta_two * beta_two)
    theta = beta_two * alpha_two / rho
    phi = alpha_one * beta_one / rho
    model_update = (phi / rho)[None, :, None] * cell_dir
    scale = jnp.sqrt(jnp.float32(CELLS))
    next_search = scale * (cell_next - (theta / rho)[None, :, None] * cell_dir)
    return (model_update, next_search)
```

```python
import functools
import math

import jax
import jax.numpy as jnp
from jax import lax
from jax.experimental import pallas as pl
from jax.experimental.pallas import tpu as pltpu
from jax.sharding import PartitionSpec as P

CB_DEV = 2
CHUNKS = 8
VMEM_LIMIT = 50 * 1024 * 1024

epsilon = 1e-06
bf16 = jnp.bfloat16
f32 = jnp.float32


def split_two(x):
    high = x.astype(bf16)
    return high, (x - high.astype(f32)).astype(bf16)


def stack_split(x):
    return jnp.concatenate(split_two(x), axis=0)


def row_squares(x):
    return jnp.sum(x * x, axis=-1, keepdims=True)


def spread(s, lanes):
    high = s.astype(bf16).astype(f32)
    rest = s - high
    middle = rest.astype(bf16).astype(f32)
    low = rest - middle
    lane = lax.broadcasted_iota(jnp.int32, (s.shape[0], lanes), 1)
    zero = jnp.zeros((s.shape[0], lanes), f32)
    out = jnp.where(lane == 0, high, zero)
    out = jnp.where(lane == 1, middle, out)
    return jnp.where(lane == 2, low, out).astype(bf16)


def dot(a, b):
    return jnp.dot(a, b, preferred_element_type=f32)


def dot_t(a, b):
    return lax.dot_general(a, b, (((1,), (1,)), ((), ())), preferred_element_type=f32)


def gather_kernel(
    row_ref, col_ref, rhs_ref, blocks_ref, high_ref, low_ref, send_ref,
    held, total, high, low, in_sem, out_sem,
):
    count, width = held.shape[0], held.shape[1]
    db = rhs_ref.shape[0]
    groups = send_ref.shape[0]
    chunk = count // CHUNKS

    def fetch(c):
        span = pl.ds(c * chunk, chunk)
        return pltpu.make_async_copy(blocks_ref.at[span], held.at[span], in_sem.at[c])

    for c in range(CHUNKS):
        fetch(c).start()

    def clear(p, carry):
        total[p] = jnp.zeros((width, width), f32)
        return carry

    lax.fori_loop(0, total.shape[0], clear, 0)

    for c in range(CHUNKS):
        fetch(c).wait()

        def add(k, carry):
            place = col_ref[k] * db + row_ref[k]
            total[place] += held[k].astype(f32)
            return carry

        lax.fori_loop(c * chunk, (c + 1) * chunk, add, 0, unroll=4)

    data = jnp.concatenate([rhs_ref[b] for b in range(db)], axis=-1)
    parts = stack_split(data)
    rows = data.shape[0]
    squares = spread(row_squares(data), width)

    def product(s, carry):
        tops, lows = [], []
        for j in range(CB_DEV):
            cell = s * CB_DEV + j
            strip = jnp.concatenate([total[cell * db + b] for b in range(db)], axis=0)
            top, rest = split_two(strip)
            high[cell] = top
            low[cell] = rest
            tops.append(top)
            lows.append(rest)
        sums = dot(parts, jnp.concatenate(tops, axis=-1)) + dot(parts, jnp.concatenate(lows, axis=-1))
        sums = sums[:rows] + sums[rows:]
        for j in range(CB_DEV):
            send_ref[s, j] = sums[:, j * width:(j + 1) * width].astype(bf16)
        send_ref[s, CB_DEV] = squares
        return carry

    lax.fori_loop(0, groups, product, 0, unroll=2)
    first = pltpu.make_async_copy(high, high_ref, out_sem.at[0])
    second = pltpu.make_async_copy(low, low_ref, out_sem.at[1])
    first.start()
    second.start()
    first.wait()
    second.wait()


def exchange_kernel(
    n, cells_root, send_one, rhs_ref, high_ref, low_ref, model_ref, search_ref,
    high, low, recv_one, send_two, recv_two, send_three, recv_three, send_four, recv_four,
    load_sem, send_sem, recv_sem,
):
    me = lax.axis_index("row")
    width = rhs_ref.shape[2]
    db = rhs_ref.shape[0]
    rows = rhs_ref.shape[1]
    loads = [
        pltpu.make_async_copy(high_ref, high, load_sem.at[0]),
        pltpu.make_async_copy(low_ref, low, load_sem.at[1]),
    ]
    for load in loads:
        load.start()

    barrier = pltpu.get_barrier_semaphore()
    for d in range(1, n):
        pl.semaphore_signal(
            barrier, inc=1, device_id={"row": lax.rem(me + d, n)}, device_id_type=pl.DeviceIdType.MESH
        )
    pl.semaphore_wait(barrier, n - 1)

    def push(phase, d, src, dst):
        return pltpu.make_async_remote_copy(
            src_ref=src,
            dst_ref=dst,
            send_sem=send_sem.at[phase, d],
            recv_sem=recv_sem.at[phase, d],
            device_id={"row": lax.rem(me + d, n)},
            device_id_type=pl.DeviceIdType.MESH,
        )

    def to(d):
        return lax.rem(me + d, n)

    def source(d):
        return lax.rem(me + n - d, n)

    def finish(copies):
        for copy in copies:
            copy.wait_send()

    def cells_of(message):
        return [message[j].astype(f32) for j in range(CB_DEV)]

    def wide(blocks):
        return jnp.concatenate(blocks, axis=-1)

    one = [push(0, d, send_one.at[to(d)], recv_one.at[d]) for d in range(1, n)]
    for copy in one:
        copy.start()
    data = wide([rhs_ref[b] for b in range(db)])
    mine = send_one[me].astype(f32)
    for d in range(1, n):
        one[d - 1].wait_recv()
        mine = mine + recv_one[d].astype(f32)
    beta_one = jnp.sqrt(jnp.sum(mine[CB_DEV], axis=-1, keepdims=True) + epsilon)
    back_one = wide([mine[j] for j in range(CB_DEV)]) / beta_one

    back_bf = back_one.astype(bf16)
    for j in range(CB_DEV):
        send_two[j] = back_bf[:, j * width:(j + 1) * width]
    send_two[CB_DEV] = spread(row_squares(back_one), width)
    two = [push(1, d, send_two, recv_two.at[d]) for d in range(1, n)]
    for copy in two:
        copy.start()
    for load in loads:
        load.wait()

    def strip(ref, s):
        return wide([ref[s * CB_DEV + j] for j in range(CB_DEV)])

    forward = dot_t(back_bf, strip(high, me)) + dot_t(back_bf, strip(low, me))
    squares = send_two[CB_DEV].astype(f32)
    for d in range(1, n):
        two[d - 1].wait_recv()
        s = source(d)
        cells = wide([recv_two[d, j] for j in range(CB_DEV)])
        forward = forward + dot_t(cells, strip(high, s)) + dot_t(cells, strip(low, s))
        squares = squares + recv_two[d, CB_DEV].astype(f32)
    alpha_one = jnp.sqrt(jnp.sum(squares, axis=-1, keepdims=True) + epsilon)
    forward = forward / alpha_one - alpha_one * (data / beta_one)

    parts = stack_split(forward)
    own_squares = spread(row_squares(forward), width)

    def terms(s):
        sums = dot(parts, strip(high, s)) + dot(parts, strip(low, s))
        return sums[:rows] + sums[rows:]

    three = []
    for d in range(1, n):
        sums = terms(to(d)).astype(bf16)
        for j in range(CB_DEV):
            send_three[d, j] = sums[:, j * width:(j + 1) * width]
        send_three[d, CB_DEV] = own_squares
        copy = push(2, d, send_three.at[d], recv_three.at[d])
        copy.start()
        three.append(copy)
    back = terms(me)
    squares = own_squares.astype(f32)
    for d in range(1, n):
        three[d - 1].wait_recv()
        back = back + wide([recv_three[d, j].astype(f32) for j in range(CB_DEV)])
        squares = squares + recv_three[d, CB_DEV].astype(f32)
    beta_two = jnp.sqrt(jnp.sum(squares, axis=-1, keepdims=True) + epsilon)
    cell_dir = back_one / alpha_one
    back_two = back / beta_two - beta_two * cell_dir

    last = row_squares(back_two)
    lane = lax.broadcasted_iota(jnp.int32, (rows // 2, width), 1)
    send_four[...] = jnp.where(
        lane == 0, last[: rows // 2], jnp.where(lane == 1, last[rows // 2:], jnp.zeros((rows // 2, width), f32))
    )
    four = [push(3, d, send_four, recv_four.at[d]) for d in range(1, n)]
    for copy in four:
        copy.start()
    rho = jnp.sqrt(alpha_one * alpha_one + beta_two * beta_two)
    phi = alpha_one * beta_one / rho
    model = (phi / rho) * cell_dir
    for j in range(CB_DEV):
        model_ref[j] = model[:, j * width:(j + 1) * width]
    finish(one)
    finish(two)
    finish(three)
    sums = send_four[...]
    for d in range(1, n):
        four[d - 1].wait_recv()
        sums = sums + recv_four[d]
    alpha_two = jnp.sqrt(jnp.concatenate([sums[:, 0:1], sums[:, 1:2]], axis=0) + epsilon)
    cell_next = back_two / alpha_two
    theta = beta_two * alpha_two / rho
    search = cells_root * (cell_next - (theta / rho) * cell_dir)
    for j in range(CB_DEV):
        search_ref[j] = search[:, j * width:(j + 1) * width]
    finish(four)


def local(rhs_data, blocks, block_row, block_col):
    n = lax.axis_size("row")
    db, rows, width = rhs_data.shape
    count = blocks.shape[0]
    cells = CB_DEV * n
    vmem = pl.BlockSpec(memory_space=pltpu.VMEM)
    smem = pl.BlockSpec(memory_space=pltpu.SMEM)
    anywhere = pl.BlockSpec(memory_space=pl.ANY)
    strip = (cells, db * width, width)
    message = (CB_DEV + 1, rows, width)
    high, low, send_one = pl.pallas_call(
        gather_kernel,
        out_shape=(
            jax.ShapeDtypeStruct(strip, bf16),
            jax.ShapeDtypeStruct(strip, bf16),
            jax.ShapeDtypeStruct((n,) + message, bf16),
        ),
        in_specs=[smem, smem, vmem, anywhere],
        out_specs=(anywhere, anywhere, vmem),
        scratch_shapes=[
            pltpu.VMEM((count, width, width), bf16),
            pltpu.VMEM((cells * db, width, width), f32),
            pltpu.VMEM(strip, bf16),
            pltpu.VMEM(strip, bf16),
            pltpu.SemaphoreType.DMA((CHUNKS,)),
            pltpu.SemaphoreType.DMA((2,)),
        ],
        compiler_params=pltpu.CompilerParams(vmem_limit_bytes=VMEM_LIMIT),
        name="strip",
    )(block_row, block_col, rhs_data, blocks)
    out = jax.ShapeDtypeStruct((CB_DEV, rows, width), f32)
    return pl.pallas_call(
        functools.partial(exchange_kernel, n, math.sqrt(float(cells * width))),
        out_shape=(out, out),
        in_specs=[vmem, vmem, anywhere, anywhere],
        out_specs=(vmem, vmem),
        scratch_shapes=[
            pltpu.VMEM(strip, bf16),
            pltpu.VMEM(strip, bf16),
            pltpu.VMEM((n,) + message, bf16),
            pltpu.VMEM(message, bf16),
            pltpu.VMEM((n,) + message, bf16),
            pltpu.VMEM((n,) + message, bf16),
            pltpu.VMEM((n,) + message, bf16),
            pltpu.VMEM((rows // 2, width), f32),
            pltpu.VMEM((n, rows // 2, width), f32),
            pltpu.SemaphoreType.DMA((2,)),
            pltpu.SemaphoreType.DMA((4, n)),
            pltpu.SemaphoreType.DMA((4, n)),
        ],
        compiler_params=pltpu.CompilerParams(
            collective_id=0, has_side_effects=True, vmem_limit_bytes=VMEM_LIMIT
        ),
        name="exchange",
    )(send_one, rhs_data, high, low)


def solution(mesh):
    in_specs = (
        P(("inv", "row"), None, None),
        P(("inv", "row"), None, None),
        P(("inv", "row")),
        P(("inv", "row")),
    )
    out_specs = (P(("inv", "row"), None, None), P(("inv", "row"), None, None))
    return jax.shard_map(local, mesh=mesh, in_specs=in_specs, out_specs=out_specs, check_vma=False)
```

```python
import functools
import math

import jax
import jax.numpy as jnp
from jax import lax
from jax.experimental import pallas as pl
from jax.experimental.pallas import tpu as pltpu
from jax.sharding import PartitionSpec as P

CB_DEV = 2
CHUNKS = 16
SPARE = 4 * 1024 * 1024
LEAST = 46 * 1024 * 1024

epsilon = 1e-06
bf16 = jnp.bfloat16
f32 = jnp.float32


def split_two(x):
    high = x.astype(bf16)
    return high, (x - high.astype(f32)).astype(bf16)


def stack_split(x):
    return jnp.concatenate(split_two(x), axis=0)


def row_squares(x):
    return jnp.sum(x * x, axis=-1, keepdims=True)


def diagonal(rows, lanes):
    row = lax.broadcasted_iota(jnp.int32, (rows, lanes), 0)
    return row == lax.broadcasted_iota(jnp.int32, (rows, lanes), 1)


def to_lanes(column, lanes):
    shape = (column.shape[0], lanes)
    placed = jnp.where(diagonal(*shape), jnp.broadcast_to(column, shape), 0.0)
    return jnp.sum(placed, axis=0, keepdims=True)


def from_lanes(line, rows):
    shape = (rows, line.shape[1])
    placed = jnp.where(diagonal(*shape), jnp.broadcast_to(line, shape), 0.0)
    return jnp.sum(placed, axis=1, keepdims=True)


def dot(a, b):
    return jnp.dot(a, b, preferred_element_type=f32)


def dot_t(a, b):
    return lax.dot_general(a, b, (((1,), (1,)), ((), ())), preferred_element_type=f32)


def gather_kernel(
    place_hbm, rhs_hbm, blocks_ref, high, low, send_ref,
    place_ref, rhs_ref, held, total, small_sem, in_sem,
):
    count, width = held.shape[0], held.shape[1]
    db = rhs_ref.shape[0]
    groups = send_ref.shape[0]
    chunk = count // CHUNKS

    def fetch(c):
        span = pl.ds(c * chunk, chunk)
        return pltpu.make_async_copy(blocks_ref.at[span], held.at[span], in_sem.at[c])

    small = [
        pltpu.make_async_copy(place_hbm, place_ref, small_sem.at[0]),
        pltpu.make_async_copy(rhs_hbm, rhs_ref, small_sem.at[1]),
    ]
    for copy in small:
        copy.start()
    for c in range(CHUNKS):
        fetch(c).start()

    def clear(p, carry):
        total[p] = jnp.zeros((width, width), f32)
        return carry

    lax.fori_loop(0, total.shape[0], clear, 0)
    for copy in small:
        copy.wait()

    for c in range(CHUNKS):
        fetch(c).wait()

        def add(k, carry):
            total[place_ref[k]] += held[k].astype(f32)
            return carry

        lax.fori_loop(c * chunk, (c + 1) * chunk, add, 0, unroll=4)

    data = jnp.concatenate([rhs_ref[b] for b in range(db)], axis=-1)
    parts = stack_split(data)
    rows = data.shape[0]

    def product(s, carry):
        tops, lows = [], []
        for j in range(CB_DEV):
            cell = s * CB_DEV + j
            strip = jnp.concatenate([total[cell * db + b] for b in range(db)], axis=0)
            top, rest = split_two(strip)
            high[cell] = top
            low[cell] = rest
            tops.append(top)
            lows.append(rest)
        sums = dot(parts, jnp.concatenate(tops, axis=-1)) + dot(parts, jnp.concatenate(lows, axis=-1))
        sums = sums[:rows] + sums[rows:]
        for j in range(CB_DEV):
            send_ref[s, j] = sums[:, j * width:(j + 1) * width].astype(bf16)
        return carry

    lax.fori_loop(0, groups, product, 0, unroll=2)


def exchange_kernel(
    n, cells_root, send_one, rhs_hbm, high, low, model_ref, search_ref,
    rhs_ref, recv_one, send_two, recv_two, send_three, recv_three, send_sums, recv_sums,
    load_sem, send_sem, recv_sem, send_sum_sem, recv_sum_sem,
):
    me = lax.axis_index("row")
    width = rhs_ref.shape[2]
    db = rhs_ref.shape[0]
    rows = rhs_ref.shape[1]
    small = pltpu.make_async_copy(rhs_hbm, rhs_ref, load_sem)
    small.start()
    barrier = pltpu.get_barrier_semaphore()
    for d in range(1, n):
        pl.semaphore_signal(
            barrier, inc=1, device_id={"row": lax.rem(me + d, n)}, device_id_type=pl.DeviceIdType.MESH
        )
    pl.semaphore_wait(barrier, n - 1)

    def push(phase, d, src, dst):
        return pltpu.make_async_remote_copy(
            src_ref=src,
            dst_ref=dst,
            send_sem=send_sem.at[phase, d],
            recv_sem=recv_sem.at[phase, d],
            device_id={"row": lax.rem(me + d, n)},
            device_id_type=pl.DeviceIdType.MESH,
        )

    def push_sums(phase, d):
        return pltpu.make_async_remote_copy(
            src_ref=send_sums.at[phase],
            dst_ref=recv_sums.at[phase, d],
            send_sem=send_sum_sem.at[phase, d],
            recv_sem=recv_sum_sem.at[phase, d],
            device_id={"row": lax.rem(me + d, n)},
            device_id_type=pl.DeviceIdType.MESH,
        )

    def start_sums(phase, column):
        send_sums[phase] = to_lanes(column, width)
        copies = [push_sums(phase, d) for d in range(1, n)]
        for copy in copies:
            copy.start()
        return copies

    def end_sums(phase, copies):
        line = send_sums[phase]
        for d in range(1, n):
            copies[d - 1].wait_recv()
            line = line + recv_sums[phase, d]
        return from_lanes(line, rows)

    def to(d):
        return lax.rem(me + d, n)

    def source(d):
        return lax.rem(me + n - d, n)

    def finish(copies):
        for copy in copies:
            copy.wait_send()

    def wide(blocks):
        return jnp.concatenate(blocks, axis=-1)

    one = [push(0, d, send_one.at[to(d)], recv_one.at[d]) for d in range(1, n)]
    for copy in one:
        copy.start()
    small.wait()
    data = wide([rhs_ref[b] for b in range(db)])
    sums_one = start_sums(0, row_squares(data))
    mine = send_one[me].astype(f32)
    for d in range(1, n):
        one[d - 1].wait_recv()
        mine = mine + recv_one[d].astype(f32)
    beta_one = jnp.sqrt(end_sums(0, sums_one) + epsilon)
    back_one = wide([mine[j] for j in range(CB_DEV)]) / beta_one

    back_bf = back_one.astype(bf16)
    for j in range(CB_DEV):
        send_two[j] = back_bf[:, j * width:(j + 1) * width]
    two = [push(1, d, send_two, recv_two.at[d]) for d in range(1, n)]
    for copy in two:
        copy.start()
    sums_two = start_sums(1, row_squares(back_one))

    def strip(ref, s):
        return wide([ref[s * CB_DEV + j] for j in range(CB_DEV)])

    forward = dot_t(back_bf, strip(high, me)) + dot_t(back_bf, strip(low, me))
    for d in range(1, n):
        two[d - 1].wait_recv()
        s = source(d)
        cells = wide([recv_two[d, j] for j in range(CB_DEV)])
        forward = forward + dot_t(cells, strip(high, s)) + dot_t(cells, strip(low, s))
    alpha_one = jnp.sqrt(end_sums(1, sums_two) + epsilon)
    forward = forward / alpha_one - alpha_one * (data / beta_one)

    parts = stack_split(forward)

    def terms(s):
        sums = dot(parts, strip(high, s)) + dot(parts, strip(low, s))
        return sums[:rows] + sums[rows:]

    three = []
    for d in range(1, n):
        sums = terms(to(d)).astype(bf16)
        for j in range(CB_DEV):
            send_three[d, j] = sums[:, j * width:(j + 1) * width]
        copy = push(2, d, send_three.at[d], recv_three.at[d])
        copy.start()
        three.append(copy)
    sums_three = start_sums(2, row_squares(forward))
    back = terms(me)
    for d in range(1, n):
        three[d - 1].wait_recv()
        back = back + wide([recv_three[d, j].astype(f32) for j in range(CB_DEV)])
    beta_two = jnp.sqrt(end_sums(2, sums_three) + epsilon)
    cell_dir = back_one / alpha_one
    back_two = back / beta_two - beta_two * cell_dir

    sums_four = start_sums(3, row_squares(back_two))
    rho = jnp.sqrt(alpha_one * alpha_one + beta_two * beta_two)
    phi = alpha_one * beta_one / rho
    model = (phi / rho) * cell_dir
    for j in range(CB_DEV):
        model_ref[j] = model[:, j * width:(j + 1) * width]
    finish(one)
    finish(two)
    finish(three)
    finish(sums_one)
    finish(sums_two)
    finish(sums_three)
    alpha_two = jnp.sqrt(end_sums(3, sums_four) + epsilon)
    cell_next = back_two / alpha_two
    theta = beta_two * alpha_two / rho
    search = cells_root * (cell_next - (theta / rho) * cell_dir)
    for j in range(CB_DEV):
        search_ref[j] = search[:, j * width:(j + 1) * width]
    finish(sums_four)


def local(rhs_data, blocks, block_row, block_col):
    n = lax.axis_size("row")
    db, rows, width = rhs_data.shape
    count = blocks.shape[0]
    cells = CB_DEV * n
    vmem = pl.BlockSpec(memory_space=pltpu.VMEM)
    anywhere = pl.BlockSpec(memory_space=pltpu.HBM)
    strip = (cells, db * width, width)
    message = (CB_DEV, rows, width)
    strip_bytes = 2 * cells * db * width * width * 2
    strip_limit = max(LEAST, SPARE + 2 * strip_bytes + count * width * width * 2)
    exchange_limit = 2 * SPARE + strip_bytes
    high, low, send_one = pl.pallas_call(
        gather_kernel,
        out_shape=(
            jax.ShapeDtypeStruct(strip, bf16),
            jax.ShapeDtypeStruct(strip, bf16),
            jax.ShapeDtypeStruct((n,) + message, bf16),
        ),
        in_specs=[anywhere] * 3,
        out_specs=(vmem, vmem, vmem),
        scratch_shapes=[
            pltpu.SMEM((count,), jnp.int32),
            pltpu.VMEM((db, rows, width), f32),
            pltpu.VMEM((count, width, width), bf16),
            pltpu.VMEM((cells * db, width, width), f32),
            pltpu.SemaphoreType.DMA((2,)),
            pltpu.SemaphoreType.DMA((CHUNKS,)),
        ],
        compiler_params=pltpu.CompilerParams(vmem_limit_bytes=strip_limit),
        name="strip",
    )(block_col * db + block_row, rhs_data, blocks)
    out = jax.ShapeDtypeStruct((CB_DEV, rows, width), f32)
    return pl.pallas_call(
        functools.partial(exchange_kernel, n, math.sqrt(float(cells * width))),
        out_shape=(out, out),
        in_specs=[vmem, anywhere, vmem, vmem],
        out_specs=(vmem, vmem),
        scratch_shapes=[
            pltpu.VMEM((db, rows, width), f32),
            pltpu.VMEM((n,) + message, bf16),
            pltpu.VMEM(message, bf16),
            pltpu.VMEM((n,) + message, bf16),
            pltpu.VMEM((n,) + message, bf16),
            pltpu.VMEM((n,) + message, bf16),
            pltpu.VMEM((4, 1, width), f32),
            pltpu.VMEM((4, n, 1, width), f32),
            pltpu.SemaphoreType.DMA(()),
            pltpu.SemaphoreType.DMA((3, n)),
            pltpu.SemaphoreType.DMA((3, n)),
            pltpu.SemaphoreType.DMA((4, n)),
            pltpu.SemaphoreType.DMA((4, n)),
        ],
        compiler_params=pltpu.CompilerParams(
            collective_id=0, has_side_effects=True, vmem_limit_bytes=exchange_limit
        ),
        name="exchange",
    )(send_one, rhs_data, high, low)


def solution(mesh):
    in_specs = (
        P(("inv", "row"), None, None),
        P(("inv", "row"), None, None),
        P(("inv", "row")),
        P(("inv", "row")),
    )
    out_specs = (P(("inv", "row"), None, None), P(("inv", "row"), None, None))
    return jax.shard_map(local, mesh=mesh, in_specs=in_specs, out_specs=out_specs, check_vma=False)
```

```python
import functools
import math

import jax
import jax.numpy as jnp
from jax import lax
from jax.experimental import pallas as pl
from jax.experimental.pallas import tpu as pltpu
from jax.sharding import PartitionSpec as P

CB_DEV = 2
CHUNKS = 16
SPARE = 4 * 1024 * 1024

epsilon = 1e-06
bf16 = jnp.bfloat16
f32 = jnp.float32


def split_two(x):
    high = x.astype(bf16)
    return high, (x - high.astype(f32)).astype(bf16)


def stack_split(x):
    return jnp.concatenate(split_two(x), axis=0)


def row_squares(x):
    return jnp.sum(x * x, axis=-1, keepdims=True)


def diagonal(rows, lanes):
    row = lax.broadcasted_iota(jnp.int32, (rows, lanes), 0)
    return row == lax.broadcasted_iota(jnp.int32, (rows, lanes), 1)


def to_lanes(column, lanes):
    shape = (column.shape[0], lanes)
    placed = jnp.where(diagonal(*shape), jnp.broadcast_to(column, shape), 0.0)
    return jnp.sum(placed, axis=0, keepdims=True)


def from_lanes(line, rows):
    shape = (rows, line.shape[1])
    placed = jnp.where(diagonal(*shape), jnp.broadcast_to(line, shape), 0.0)
    return jnp.sum(placed, axis=1, keepdims=True)


def dot(a, b):
    return jnp.dot(a, b, preferred_element_type=f32)


def dot_t(a, b):
    return lax.dot_general(a, b, (((1,), (1,)), ((), ())), preferred_element_type=f32)


def kernel(
    n, cells_root, table_hbm, rhs_hbm, blocks_ref, model_ref, search_ref,
    table, rhs_ref, held, total, high, low,
    send_one, recv_one, send_two, recv_two, send_three, recv_three, send_sums, recv_sums,
    small_sem, in_sem, send_sem, recv_sem, send_sum_sem, recv_sum_sem,
):
    me = lax.axis_index("row")
    db, rows, width = rhs_ref.shape
    count = held.shape[0]
    chunk = count // CHUNKS

    def fetch(c):
        span = pl.ds(c * chunk, chunk)
        return pltpu.make_async_copy(blocks_ref.at[span], held.at[span], in_sem.at[c])

    small = [
        pltpu.make_async_copy(table_hbm, table, small_sem.at[0]),
        pltpu.make_async_copy(rhs_hbm, rhs_ref, small_sem.at[1]),
    ]
    for copy in small:
        copy.start()
    for c in range(CHUNKS):
        fetch(c).start()

    barrier = pltpu.get_barrier_semaphore()
    for d in range(1, n):
        pl.semaphore_signal(
            barrier, inc=1, device_id={"row": lax.rem(me + d, n)}, device_id_type=pl.DeviceIdType.MESH
        )
    total[count] = jnp.zeros((width, width), f32)
    for copy in small:
        copy.wait()

    for c in range(CHUNKS):
        fetch(c).wait()

        def add(k, carry):
            total[k] = total[table[k]] + held[k].astype(f32)
            return carry

        lax.fori_loop(c * chunk, (c + 1) * chunk, add, 0, unroll=4)

    def push(phase, d, src, dst):
        return pltpu.make_async_remote_copy(
            src_ref=src,
            dst_ref=dst,
            send_sem=send_sem.at[phase, d],
            recv_sem=recv_sem.at[phase, d],
            device_id={"row": lax.rem(me + d, n)},
            device_id_type=pl.DeviceIdType.MESH,
        )

    def push_sums(phase, d):
        return pltpu.make_async_remote_copy(
            src_ref=send_sums.at[phase],
            dst_ref=recv_sums.at[phase, d],
            send_sem=send_sum_sem.at[phase, d],
            recv_sem=recv_sum_sem.at[phase, d],
            device_id={"row": lax.rem(me + d, n)},
            device_id_type=pl.DeviceIdType.MESH,
        )

    def start_sums(phase, column):
        send_sums[phase] = to_lanes(column, width)
        copies = [push_sums(phase, d) for d in range(1, n)]
        for copy in copies:
            copy.start()
        return copies

    def end_sums(phase, copies):
        line = send_sums[phase]
        for d in range(1, n):
            copies[d - 1].wait_recv()
            line = line + recv_sums[phase, d]
        return from_lanes(line, rows)

    def to(d):
        return lax.rem(me + d, n)

    def source(d):
        return lax.rem(me + n - d, n)

    def finish(copies):
        for copy in copies:
            copy.wait_send()

    def wide(blocks):
        return jnp.concatenate(blocks, axis=-1)

    data = wide([rhs_ref[b] for b in range(db)])
    data_parts = stack_split(data)

    def product(s, carry):
        tops, lows = [], []
        for j in range(CB_DEV):
            cell = s * CB_DEV + j
            dense = jnp.concatenate([total[table[count + cell * db + b]] for b in range(db)], axis=0)
            top, rest = split_two(dense)
            high[cell] = top
            low[cell] = rest
            tops.append(top)
            lows.append(rest)
        sums = dot(data_parts, wide(tops)) + dot(data_parts, wide(lows))
        sums = sums[:rows] + sums[rows:]
        for j in range(CB_DEV):
            send_one[s, j] = sums[:, j * width:(j + 1) * width].astype(bf16)
        return carry

    lax.fori_loop(0, n, product, 0, unroll=2)
    pl.semaphore_wait(barrier, n - 1)
    one = [push(0, d, send_one.at[to(d)], recv_one.at[d]) for d in range(1, n)]
    for copy in one:
        copy.start()
    sums_one = start_sums(0, row_squares(data))
    mine = send_one[me].astype(f32)
    for d in range(1, n):
        one[d - 1].wait_recv()
        mine = mine + recv_one[d].astype(f32)
    beta_one = jnp.sqrt(end_sums(0, sums_one) + epsilon)
    back_one = wide([mine[j] for j in range(CB_DEV)]) / beta_one

    back_bf = back_one.astype(bf16)
    for j in range(CB_DEV):
        send_two[j] = back_bf[:, j * width:(j + 1) * width]
    two = [push(1, d, send_two, recv_two.at[d]) for d in range(1, n)]
    for copy in two:
        copy.start()
    sums_two = start_sums(1, row_squares(back_one))

    def strip(ref, s):
        return wide([ref[s * CB_DEV + j] for j in range(CB_DEV)])

    forward = dot_t(back_bf, strip(high, me)) + dot_t(back_bf, strip(low, me))
    for d in range(1, n):
        two[d - 1].wait_recv()
        s = source(d)
        cells = wide([recv_two[d, j] for j in range(CB_DEV)])
        forward = forward + dot_t(cells, strip(high, s)) + dot_t(cells, strip(low, s))
    alpha_one = jnp.sqrt(end_sums(1, sums_two) + epsilon)
    forward = forward / alpha_one - alpha_one * (data / beta_one)

    parts = stack_split(forward)

    def terms(s):
        sums = dot(parts, strip(high, s)) + dot(parts, strip(low, s))
        return sums[:rows] + sums[rows:]

    three = []
    for d in range(1, n):
        sums = terms(to(d)).astype(bf16)
        for j in range(CB_DEV):
            send_three[d, j] = sums[:, j * width:(j + 1) * width]
        copy = push(2, d, send_three.at[d], recv_three.at[d])
        copy.start()
        three.append(copy)
    sums_three = start_sums(2, row_squares(forward))
    back = terms(me)
    for d in range(1, n):
        three[d - 1].wait_recv()
        back = back + wide([recv_three[d, j].astype(f32) for j in range(CB_DEV)])
    beta_two = jnp.sqrt(end_sums(2, sums_three) + epsilon)
    cell_dir = back_one / alpha_one
    back_two = back / beta_two - beta_two * cell_dir

    sums_four = start_sums(3, row_squares(back_two))
    rho = jnp.sqrt(alpha_one * alpha_one + beta_two * beta_two)
    phi = alpha_one * beta_one / rho
    model = (phi / rho) * cell_dir
    for j in range(CB_DEV):
        model_ref[j] = model[:, j * width:(j + 1) * width]
    finish(one)
    finish(two)
    finish(three)
    finish(sums_one)
    finish(sums_two)
    finish(sums_three)
    alpha_two = jnp.sqrt(end_sums(3, sums_four) + epsilon)
    cell_next = back_two / alpha_two
    theta = beta_two * alpha_two / rho
    search = cells_root * (cell_next - (theta / rho) * cell_dir)
    for j in range(CB_DEV):
        search_ref[j] = search[:, j * width:(j + 1) * width]
    finish(sums_four)


def local(rhs_data, blocks, block_row, block_col):
    n = lax.axis_size("row")
    db, rows, width = rhs_data.shape
    count = blocks.shape[0]
    cells = CB_DEV * n
    place = block_col * db + block_row
    k = jnp.arange(count, dtype=jnp.int32)
    asked = jnp.concatenate([place, jnp.arange(cells * db, dtype=jnp.int32)])
    before = jnp.concatenate([k, jnp.full((cells * db,), count, jnp.int32)])
    hit = (place[None, :] == asked[:, None]) & (k[None, :] < before[:, None])
    table = jnp.max(jnp.where(hit, k[None, :], -1), axis=1)
    table = jnp.where(table < 0, count, table)

    vmem = pl.BlockSpec(memory_space=pltpu.VMEM)
    anywhere = pl.BlockSpec(memory_space=pltpu.HBM)
    strip = (cells, db * width, width)
    message = (CB_DEV, rows, width)
    strip_bytes = 2 * cells * db * width * width * 2
    limit = SPARE + strip_bytes + 3 * count * width * width * 2
    out = jax.ShapeDtypeStruct((CB_DEV, rows, width), f32)
    return pl.pallas_call(
        functools.partial(kernel, n, math.sqrt(float(cells * width))),
        out_shape=(out, out),
        in_specs=[anywhere] * 3,
        out_specs=(vmem, vmem),
        scratch_shapes=[
            pltpu.SMEM(table.shape, jnp.int32),
            pltpu.VMEM((db, rows, width), f32),
            pltpu.VMEM((count, width, width), bf16),
            pltpu.VMEM((count + 1, width, width), f32),
            pltpu.VMEM(strip, bf16),
            pltpu.VMEM(strip, bf16),
            pltpu.VMEM((n,) + message, bf16),
            pltpu.VMEM((n,) + message, bf16),
            pltpu.VMEM(message, bf16),
            pltpu.VMEM((n,) + message, bf16),
            pltpu.VMEM((n,) + message, bf16),
            pltpu.VMEM((n,) + message, bf16),
            pltpu.VMEM((4, 1, width), f32),
            pltpu.VMEM((4, n, 1, width), f32),
            pltpu.SemaphoreType.DMA((2,)),
            pltpu.SemaphoreType.DMA((CHUNKS,)),
            pltpu.SemaphoreType.DMA((3, n)),
            pltpu.SemaphoreType.DMA((3, n)),
            pltpu.SemaphoreType.DMA((4, n)),
            pltpu.SemaphoreType.DMA((4, n)),
        ],
        compiler_params=pltpu.CompilerParams(
            collective_id=0, has_side_effects=True, vmem_limit_bytes=limit
        ),
        name="iteration",
    )(table, rhs_data, blocks)


def solution(mesh):
    in_specs = (
        P(("inv", "row"), None, None),
        P(("inv", "row"), None, None),
        P(("inv", "row")),
        P(("inv", "row")),
    )
    out_specs = (P(("inv", "row"), None, None), P(("inv", "row"), None, None))
    return jax.shard_map(local, mesh=mesh, in_specs=in_specs, out_specs=out_specs, check_vma=False)
```

```python
import functools
import math

import jax
import jax.numpy as jnp
from jax import lax
from jax.experimental import pallas as pl
from jax.experimental.pallas import tpu as pltpu
from jax.sharding import PartitionSpec as P

CB_DEV = 2
CHUNKS = 16
SPARE = 4 * 1024 * 1024

epsilon = 1e-06
bf16 = jnp.bfloat16
f32 = jnp.float32


def split_two(x):
    high = x.astype(bf16)
    return high, (x - high.astype(f32)).astype(bf16)


def stack_split(x):
    return jnp.concatenate(split_two(x), axis=0)


def row_squares(x):
    return jnp.sum(x * x, axis=-1, keepdims=True)


def diagonal(rows, lanes):
    row = lax.broadcasted_iota(jnp.int32, (rows, lanes), 0)
    return row == lax.broadcasted_iota(jnp.int32, (rows, lanes), 1)


def to_lanes(column, lanes):
    shape = (column.shape[0], lanes)
    placed = jnp.where(diagonal(*shape), jnp.broadcast_to(column, shape), 0.0)
    return jnp.sum(placed, axis=0, keepdims=True)


def from_lanes(line, rows):
    shape = (rows, line.shape[1])
    placed = jnp.where(diagonal(*shape), jnp.broadcast_to(line, shape), 0.0)
    return jnp.sum(placed, axis=1, keepdims=True)


def dot(a, b):
    return jnp.dot(a, b, preferred_element_type=f32)


def dot_t(a, b):
    return lax.dot_general(a, b, (((1,), (1,)), ((), ())), preferred_element_type=f32)


def kernel(
    n, cells_root, table_hbm, rhs_hbm, blocks_ref, model_ref, search_ref,
    table, rhs_ref, held, total, high, low,
    send_one, recv_one, send_two, recv_two, send_three, recv_three, send_sums, recv_sums,
    small_sem, in_sem, send_sem, recv_sem, send_sum_sem, recv_sum_sem,
):
    me = lax.axis_index("row")
    db, rows, width = rhs_ref.shape
    count = held.shape[0]
    chunk = count // CHUNKS

    def to(d):
        index, bit = me, 1
        while bit < n:
            if d & bit:
                index = index + bit * (1 - 2 * lax.rem(me // bit, 2))
            bit *= 2
        return index

    far_first = range(n - 1, 0, -1)

    def fetch(c):
        span = pl.ds(c * chunk, chunk)
        return pltpu.make_async_copy(blocks_ref.at[span], held.at[span], in_sem.at[c])

    small = [
        pltpu.make_async_copy(table_hbm, table, small_sem.at[0]),
        pltpu.make_async_copy(rhs_hbm, rhs_ref, small_sem.at[1]),
    ]
    for copy in small:
        copy.start()
    for c in range(CHUNKS):
        fetch(c).start()

    barrier = pltpu.get_barrier_semaphore()
    for d in range(1, n):
        pl.semaphore_signal(
            barrier, inc=1, device_id={"row": to(d)}, device_id_type=pl.DeviceIdType.MESH
        )
    total[count] = jnp.zeros((width, width), f32)
    for copy in small:
        copy.wait()

    for c in range(CHUNKS):
        fetch(c).wait()

        def add(k, carry):
            total[k] = total[table[k]] + held[k].astype(f32)
            return carry

        lax.fori_loop(c * chunk, (c + 1) * chunk, add, 0, unroll=4)

    def push(phase, d, src, dst):
        return pltpu.make_async_remote_copy(
            src_ref=src,
            dst_ref=dst,
            send_sem=send_sem.at[phase, d],
            recv_sem=recv_sem.at[phase, d],
            device_id={"row": to(d)},
            device_id_type=pl.DeviceIdType.MESH,
        )

    def push_sums(phase, d):
        return pltpu.make_async_remote_copy(
            src_ref=send_sums.at[phase],
            dst_ref=recv_sums.at[phase, d],
            send_sem=send_sum_sem.at[phase, d],
            recv_sem=recv_sum_sem.at[phase, d],
            device_id={"row": to(d)},
            device_id_type=pl.DeviceIdType.MESH,
        )

    def start_sums(phase, column):
        send_sums[phase] = to_lanes(column, width)
        copies = [push_sums(phase, d) for d in far_first]
        for copy in copies:
            copy.start()
        return copies

    def end_sums(phase, copies):
        line = send_sums[phase]
        for d in range(1, n):
            copies[n - 1 - d].wait_recv()
            line = line + recv_sums[phase, d]
        return from_lanes(line, rows)

    def finish(copies):
        for copy in copies:
            copy.wait_send()

    def wide(blocks):
        return jnp.concatenate(blocks, axis=-1)

    data = wide([rhs_ref[b] for b in range(db)])
    data_parts = stack_split(data)

    def product(s):
        tops, lows = [], []
        for j in range(CB_DEV):
            cell = s * CB_DEV + j
            dense = jnp.concatenate([total[table[count + cell * db + b]] for b in range(db)], axis=0)
            top, rest = split_two(dense)
            high[cell] = top
            low[cell] = rest
            tops.append(top)
            lows.append(rest)
        sums = dot(data_parts, wide(tops)) + dot(data_parts, wide(lows))
        return sums[:rows] + sums[rows:]

    pl.semaphore_wait(barrier, n - 1)
    sums_one = start_sums(0, row_squares(data))
    one = {}
    for d in far_first:
        sums = product(to(d)).astype(bf16)
        for j in range(CB_DEV):
            send_one[d, j] = sums[:, j * width:(j + 1) * width]
        one[d] = push(0, d, send_one.at[d], recv_one.at[d])
        one[d].start()
    mine = product(me)
    for d in range(1, n):
        one[d].wait_recv()
        mine = mine + wide([recv_one[d, j].astype(f32) for j in range(CB_DEV)])
    beta_one = jnp.sqrt(end_sums(0, sums_one) + epsilon)
    back_one = mine / beta_one

    back_bf = back_one.astype(bf16)
    for j in range(CB_DEV):
        send_two[j] = back_bf[:, j * width:(j + 1) * width]
    two = {d: push(1, d, send_two, recv_two.at[d]) for d in far_first}
    for copy in two.values():
        copy.start()
    sums_two = start_sums(1, row_squares(back_one))

    def strip(ref, s):
        return wide([ref[s * CB_DEV + j] for j in range(CB_DEV)])

    forward = dot_t(back_bf, strip(high, me)) + dot_t(back_bf, strip(low, me))
    for d in range(1, n):
        two[d].wait_recv()
        s = to(d)
        cells = wide([recv_two[d, j] for j in range(CB_DEV)])
        forward = forward + dot_t(cells, strip(high, s)) + dot_t(cells, strip(low, s))
    alpha_one = jnp.sqrt(end_sums(1, sums_two) + epsilon)
    forward = forward / alpha_one - alpha_one * (data / beta_one)

    parts = stack_split(forward)

    def terms(s):
        sums = dot(parts, strip(high, s)) + dot(parts, strip(low, s))
        return sums[:rows] + sums[rows:]

    sums_three = start_sums(2, row_squares(forward))
    three = {}
    for d in far_first:
        sums = terms(to(d)).astype(bf16)
        for j in range(CB_DEV):
            send_three[d, j] = sums[:, j * width:(j + 1) * width]
        three[d] = push(2, d, send_three.at[d], recv_three.at[d])
        three[d].start()
    back = terms(me)
    for d in range(1, n):
        three[d].wait_recv()
        back = back + wide([recv_three[d, j].astype(f32) for j in range(CB_DEV)])
    beta_two = jnp.sqrt(end_sums(2, sums_three) + epsilon)
    cell_dir = back_one / alpha_one
    back_two = back / beta_two - beta_two * cell_dir

    sums_four = start_sums(3, row_squares(back_two))
    rho = jnp.sqrt(alpha_one * alpha_one + beta_two * beta_two)
    phi = alpha_one * beta_one / rho
    model = (phi / rho) * cell_dir
    for j in range(CB_DEV):
        model_ref[j] = model[:, j * width:(j + 1) * width]
    finish(one.values())
    finish(two.values())
    finish(three.values())
    finish(sums_one)
    finish(sums_two)
    finish(sums_three)
    alpha_two = jnp.sqrt(end_sums(3, sums_four) + epsilon)
    cell_next = back_two / alpha_two
    theta = beta_two * alpha_two / rho
    search = cells_root * (cell_next - (theta / rho) * cell_dir)
    for j in range(CB_DEV):
        search_ref[j] = search[:, j * width:(j + 1) * width]
    finish(sums_four)


def local(rhs_data, blocks, block_row, block_col):
    n = lax.axis_size("row")
    db, rows, width = rhs_data.shape
    count = blocks.shape[0]
    cells = CB_DEV * n
    place = block_col * db + block_row
    k = jnp.arange(count, dtype=jnp.int32)
    asked = jnp.concatenate([place, jnp.arange(cells * db, dtype=jnp.int32)])
    before = jnp.concatenate([k, jnp.full((cells * db,), count, jnp.int32)])
    hit = (place[None, :] == asked[:, None]) & (k[None, :] < before[:, None])
    table = jnp.max(jnp.where(hit, k[None, :], -1), axis=1)
    table = jnp.where(table < 0, count, table)

    vmem = pl.BlockSpec(memory_space=pltpu.VMEM)
    anywhere = pl.BlockSpec(memory_space=pltpu.HBM)
    strip = (cells, db * width, width)
    message = (CB_DEV, rows, width)
    strip_bytes = 2 * cells * db * width * width * 2
    limit = SPARE + strip_bytes + 3 * count * width * width * 2
    out = jax.ShapeDtypeStruct((CB_DEV, rows, width), f32)
    return pl.pallas_call(
        functools.partial(kernel, n, math.sqrt(float(cells * width))),
        out_shape=(out, out),
        in_specs=[anywhere] * 3,
        out_specs=(vmem, vmem),
        scratch_shapes=[
            pltpu.SMEM(table.shape, jnp.int32),
            pltpu.VMEM((db, rows, width), f32),
            pltpu.VMEM((count, width, width), bf16),
            pltpu.VMEM((count + 1, width, width), f32),
            pltpu.VMEM(strip, bf16),
            pltpu.VMEM(strip, bf16),
            pltpu.VMEM((n,) + message, bf16),
            pltpu.VMEM((n,) + message, bf16),
            pltpu.VMEM(message, bf16),
            pltpu.VMEM((n,) + message, bf16),
            pltpu.VMEM((n,) + message, bf16),
            pltpu.VMEM((n,) + message, bf16),
            pltpu.VMEM((4, 1, width), f32),
            pltpu.VMEM((4, n, 1, width), f32),
            pltpu.SemaphoreType.DMA((2,)),
            pltpu.SemaphoreType.DMA((CHUNKS,)),
            pltpu.SemaphoreType.DMA((3, n)),
            pltpu.SemaphoreType.DMA((3, n)),
            pltpu.SemaphoreType.DMA((4, n)),
            pltpu.SemaphoreType.DMA((4, n)),
        ],
        compiler_params=pltpu.CompilerParams(
            collective_id=0, has_side_effects=True, vmem_limit_bytes=limit
        ),
        name="iteration",
    )(table, rhs_data, blocks)


def solution(mesh):
    in_specs = (
        P(("inv", "row"), None, None),
        P(("inv", "row"), None, None),
        P(("inv", "row")),
        P(("inv", "row")),
    )
    out_specs = (P(("inv", "row"), None, None), P(("inv", "row"), None, None))
    return jax.shard_map(local, mesh=mesh, in_specs=in_specs, out_specs=out_specs, check_vma=False)
```

```python
import functools
import math

import jax
import jax.numpy as jnp
from jax import lax
from jax.experimental import pallas as pl
from jax.experimental.pallas import tpu as pltpu
from jax.sharding import PartitionSpec as P

CB_DEV = 2
CHUNKS = 16
SPARE = 4 * 1024 * 1024

epsilon = 1e-06
bf16 = jnp.bfloat16
f32 = jnp.float32


def split_two(x):
    high = x.astype(bf16)
    return high, (x - high.astype(f32)).astype(bf16)


def stack_split(x):
    return jnp.concatenate(split_two(x), axis=0)


def row_squares(x):
    return jnp.sum(x * x, axis=-1, keepdims=True)


def diagonal(rows, lanes):
    row = lax.broadcasted_iota(jnp.int32, (rows, lanes), 0)
    return row == lax.broadcasted_iota(jnp.int32, (rows, lanes), 1)


def to_lanes(column, lanes):
    shape = (column.shape[0], lanes)
    placed = jnp.where(diagonal(*shape), jnp.broadcast_to(column, shape), 0.0)
    return jnp.sum(placed, axis=0, keepdims=True)


def from_lanes(line, rows):
    shape = (rows, line.shape[1])
    placed = jnp.where(diagonal(*shape), jnp.broadcast_to(line, shape), 0.0)
    return jnp.sum(placed, axis=1, keepdims=True)


def dot(a, b):
    return jnp.dot(a, b, preferred_element_type=f32)


def dot_t(a, b):
    return lax.dot_general(a, b, (((1,), (1,)), ((), ())), preferred_element_type=f32)


def kernel(
    n, table_hbm, rhs_hbm, blocks_ref, model_ref, search_ref, factor_ref,
    table, rhs_ref, held, total, high, low,
    send_one, recv_one, send_two, recv_two, send_three, recv_three, send_sums, recv_sums,
    small_sem, in_sem, send_sem, recv_sem, send_sum_sem, recv_sum_sem,
):
    me = lax.axis_index("row")
    db, rows, width = rhs_ref.shape
    count = held.shape[0]
    chunk = count // CHUNKS

    def to(d):
        index, bit = me, 1
        while bit < n:
            if d & bit:
                index = index + bit * (1 - 2 * lax.rem(me // bit, 2))
            bit *= 2
        return index

    far_first = range(n - 1, 0, -1)

    def fetch(c):
        span = pl.ds(c * chunk, chunk)
        return pltpu.make_async_copy(blocks_ref.at[span], held.at[span], in_sem.at[c])

    small = [
        pltpu.make_async_copy(table_hbm, table, small_sem.at[0]),
        pltpu.make_async_copy(rhs_hbm, rhs_ref, small_sem.at[1]),
    ]
    for copy in small:
        copy.start()
    for c in range(CHUNKS):
        fetch(c).start()

    barrier = pltpu.get_barrier_semaphore()
    for d in range(1, n):
        pl.semaphore_signal(
            barrier, inc=1, device_id={"row": to(d)}, device_id_type=pl.DeviceIdType.MESH
        )
    total[count] = jnp.zeros((width, width), f32)
    for copy in small:
        copy.wait()

    for c in range(CHUNKS):
        fetch(c).wait()

        def add(k, carry):
            total[k] = total[table[0, k]] + held[k].astype(f32)
            return carry

        lax.fori_loop(c * chunk, (c + 1) * chunk, add, 0, unroll=4)

    def push(phase, d, src, dst):
        return pltpu.make_async_remote_copy(
            src_ref=src,
            dst_ref=dst,
            send_sem=send_sem.at[phase, d],
            recv_sem=recv_sem.at[phase, d],
            device_id={"row": to(d)},
            device_id_type=pl.DeviceIdType.MESH,
        )

    def push_sums(phase, d):
        return pltpu.make_async_remote_copy(
            src_ref=send_sums.at[phase],
            dst_ref=recv_sums.at[phase, d],
            send_sem=send_sum_sem.at[phase, d],
            recv_sem=recv_sum_sem.at[phase, d],
            device_id={"row": to(d)},
            device_id_type=pl.DeviceIdType.MESH,
        )

    def start_sums(phase, column):
        send_sums[phase] = to_lanes(column, width)
        copies = [push_sums(phase, d) for d in far_first]
        for copy in copies:
            copy.start()
        return copies

    def end_sums(phase, copies):
        line = send_sums[phase]
        for d in range(1, n):
            copies[n - 1 - d].wait_recv()
            line = line + recv_sums[phase, d]
        return from_lanes(line, rows)

    def finish(copies):
        for copy in copies:
            copy.wait_send()

    def wide(blocks):
        return jnp.concatenate(blocks, axis=-1)

    data = wide([rhs_ref[b] for b in range(db)])
    data_parts = stack_split(data)

    def product(s):
        tops, lows = [], []
        for j in range(CB_DEV):
            cell = s * CB_DEV + j
            dense = jnp.concatenate([total[table[1, cell * db + b]] for b in range(db)], axis=0)
            top, rest = split_two(dense)
            high[cell] = top
            low[cell] = rest
            tops.append(top)
            lows.append(rest)
        sums = dot(data_parts, wide(tops)) + dot(data_parts, wide(lows))
        return sums[:rows] + sums[rows:]

    pl.semaphore_wait(barrier, n - 1)
    sums_one = start_sums(0, row_squares(data))
    one = {}
    for d in far_first:
        sums = product(to(d)).astype(bf16)
        for j in range(CB_DEV):
            send_one[d, j] = sums[:, j * width:(j + 1) * width]
        one[d] = push(0, d, send_one.at[d], recv_one.at[d])
        one[d].start()
    mine = product(me)
    for d in range(1, n):
        one[d].wait_recv()
        mine = mine + wide([recv_one[d, j].astype(f32) for j in range(CB_DEV)])
    beta_one = jnp.sqrt(end_sums(0, sums_one) + epsilon)
    back_one = mine / beta_one

    back_bf = back_one.astype(bf16)
    for j in range(CB_DEV):
        send_two[j] = back_bf[:, j * width:(j + 1) * width]
    two = {d: push(1, d, send_two, recv_two.at[d]) for d in far_first}
    for copy in two.values():
        copy.start()
    sums_two = start_sums(1, row_squares(back_one))

    def strip(ref, s):
        return wide([ref[s * CB_DEV + j] for j in range(CB_DEV)])

    forward = dot_t(back_bf, strip(high, me)) + dot_t(back_bf, strip(low, me))
    for d in range(1, n):
        two[d].wait_recv()
        s = to(d)
        cells = wide([recv_two[d, j] for j in range(CB_DEV)])
        forward = forward + dot_t(cells, strip(high, s)) + dot_t(cells, strip(low, s))
    alpha_one = jnp.sqrt(end_sums(1, sums_two) + epsilon)
    forward = forward / alpha_one - alpha_one * (data / beta_one)

    parts = stack_split(forward)

    def terms(s):
        sums = dot(parts, strip(high, s)) + dot(parts, strip(low, s))
        return sums[:rows] + sums[rows:]

    sums_three = start_sums(2, row_squares(forward))
    three = {}
    for d in far_first:
        sums = terms(to(d)).astype(bf16)
        for j in range(CB_DEV):
            send_three[d, j] = sums[:, j * width:(j + 1) * width]
        three[d] = push(2, d, send_three.at[d], recv_three.at[d])
        three[d].start()
    back = terms(me)
    for d in range(1, n):
        three[d].wait_recv()
        back = back + wide([recv_three[d, j].astype(f32) for j in range(CB_DEV)])
    beta_two = jnp.sqrt(end_sums(2, sums_three) + epsilon)
    cell_dir = back_one / alpha_one
    back_two = back / beta_two - beta_two * cell_dir

    sums_four = start_sums(3, row_squares(back_two))
    rho = jnp.sqrt(alpha_one * alpha_one + beta_two * beta_two)
    phi = alpha_one * beta_one / rho
    model = (phi / rho) * cell_dir
    for j in range(CB_DEV):
        model_ref[j] = cell_dir[:, j * width:(j + 1) * width]
    finish(one.values())
    finish(two.values())
    finish(three.values())
    finish(sums_one)
    finish(sums_two)
    finish(sums_three)
    alpha_two = jnp.sqrt(end_sums(3, sums_four) + epsilon)
    cell_next = back_two / alpha_two
    theta = beta_two * alpha_two / rho
    for j in range(CB_DEV):
        search_ref[j] = cell_next[:, j * width:(j + 1) * width]
    factor_ref[0] = jnp.broadcast_to(phi / rho, (rows, width))
    factor_ref[1] = jnp.broadcast_to(theta / rho, (rows, width))
    finish(sums_four)


def local(rhs_data, blocks, block_row, block_col):
    n = lax.axis_size("row")
    db, rows, width = rhs_data.shape
    count = blocks.shape[0]
    cells = CB_DEV * n
    place = block_col * db + block_row
    k = jnp.arange(count, dtype=jnp.int32)
    slots = max(count, cells * db)
    asked = jnp.pad(place, (0, slots - count), constant_values=-1)
    slot = jnp.arange(slots, dtype=jnp.int32)
    earlier = (place[None, :] == asked[:, None]) & (k[None, :] < slot[:, None])
    here = place[None, :] == slot[:, None]
    hit = jnp.stack([earlier, here])
    table = jnp.max(jnp.where(hit, k[None, None, :], -1), axis=2)
    table = jnp.where(table < 0, count, table)

    vmem = pl.BlockSpec(memory_space=pltpu.VMEM)
    anywhere = pl.BlockSpec(memory_space=pltpu.HBM)
    strip = (cells, db * width, width)
    message = (CB_DEV, rows, width)
    strip_bytes = 2 * cells * db * width * width * 2
    limit = SPARE + strip_bytes + 3 * count * width * width * 2
    out = jax.ShapeDtypeStruct((CB_DEV, rows, width), f32)
    cell_dir, cell_next, factors = pl.pallas_call(
        functools.partial(kernel, n),
        out_shape=(out, out, jax.ShapeDtypeStruct((2, rows, width), f32)),
        in_specs=[anywhere] * 3,
        out_specs=(vmem, vmem, vmem),
        scratch_shapes=[
            pltpu.SMEM(table.shape, jnp.int32),
            pltpu.VMEM((db, rows, width), f32),
            pltpu.VMEM((count, width, width), bf16),
            pltpu.VMEM((count + 1, width, width), f32),
            pltpu.VMEM(strip, bf16),
            pltpu.VMEM(strip, bf16),
            pltpu.VMEM((n,) + message, bf16),
            pltpu.VMEM((n,) + message, bf16),
            pltpu.VMEM(message, bf16),
            pltpu.VMEM((n,) + message, bf16),
            pltpu.VMEM((n,) + message, bf16),
            pltpu.VMEM((n,) + message, bf16),
            pltpu.VMEM((4, 1, width), f32),
            pltpu.VMEM((4, n, 1, width), f32),
            pltpu.SemaphoreType.DMA((2,)),
            pltpu.SemaphoreType.DMA((CHUNKS,)),
            pltpu.SemaphoreType.DMA((3, n)),
            pltpu.SemaphoreType.DMA((3, n)),
            pltpu.SemaphoreType.DMA((4, n)),
            pltpu.SemaphoreType.DMA((4, n)),
        ],
        compiler_params=pltpu.CompilerParams(
            collective_id=0, has_side_effects=True, vmem_limit_bytes=limit
        ),
        name="iteration",
    )(table, rhs_data, blocks)
    scale = jnp.float32(math.sqrt(float(cells * width)))
    model_update = factors[0][None] * cell_dir
    next_search = scale * (cell_next - factors[1][None] * cell_dir)
    return model_update, next_search


def solution(mesh):
    in_specs = (
        P(("inv", "row"), None, None),
        P(("inv", "row"), None, None),
        P(("inv", "row")),
        P(("inv", "row")),
    )
    out_specs = (P(("inv", "row"), None, None), P(("inv", "row"), None, None))
    return jax.shard_map(local, mesh=mesh, in_specs=in_specs, out_specs=out_specs, check_vma=False)
```
